32 devices in a mesh: orient: 8 (over z, x), frame: 4 (over y, core).
Axes of the slice: x: 2, y: 2, z: 4, core: 2. Of those that a mesh axis runs over, the one named last changes fastest.
Arguments:
- volume: float32 [507904], P('orient'), may hold values from 0.1 to 10
- voxel_index: int32 [16, 1024], P(None, 'orient'), may hold values from 0 to 63487
- pixel_index: int32 [16, 1024], P('orient'), may hold values from 0 to 4095
- weights: bfloat16 [16, 1024], P('orient'), may hold values from 0.049804688 to 0.5
- background: float32 [4096], replicated, may hold values from 0.2 to 1
- counts: int32 [1024, 4096], P('frame'), may hold values from 0 to 16, as said below
Outputs:
- new_volume: float32 [507904], P('orient')
- probs: float32 [16, 1024], P('orient', 'frame')
The draws below stay inside these ranges and needn't reach their ends.
Inputs may be any that keep to these rules, and one draw needn't show every extreme that they name: Photon counts; frames differ in their mean count.
All inputs are finite; a program needn't handle non-finite values.
Results may differ from the reference program's by a relative error of at most 0.0003.
Values sent between devices are 32-bit elements; how exact they have to be, the bound alone decides.
A program may use at most 64 MiB of HBM per device.

```python
import math
import jax
import jax.numpy as jnp
from jax import lax

PIX = 4096
VOX_DEV = 63488
ENTRIES = 128
SLABS = 8
VOXELS = 507904
ORIENTS = 16
FRAMES = 1024


def draw_counts(key, part):
    key = jax.random.fold_in(key, 11)
    key_level, key_count = jax.random.split(key)
    level = jax.random.randint(key_level, (FRAMES, 1), 0, 8)
    frame_ids = jnp.arange(FRAMES, dtype=jnp.int32)[:, None]
    level = jnp.where(frame_ids == 0, 7, level)
    level = jnp.where(frame_ids == 1, 0, level)
    counts = jax.random.randint(key_count, (FRAMES, PIX), 0, 2 * level + 3)
    pixel_ids = jnp.arange(PIX, dtype=jnp.int32)[None, :]
    counts = jnp.where((frame_ids == 0) & (pixel_ids == 0), 16, counts)
    return counts.astype(jnp.int32)


def with_ends(values, stream_key, least, top_value):
    extent = values.shape
    place = [jax.random.randint(jax.random.fold_in(stream_key, axis), (), 0, extent[axis]) for axis in range(len(extent))]
    values = values.at[tuple(place)].set(least)
    longest = extent.index(max(extent))
    place[longest] = (place[longest] + 1) % extent[longest]
    return values.at[tuple(place)].set(top_value)


def level_of(stream_key, shape, cuts, smallest, top_value):
    gain = 1.0
    for axis_at, shards_of in cuts:
        steps = jax.random.uniform(jax.random.fold_in(jax.random.fold_in(stream_key, 6), axis_at), (shards_of,), jnp.float32, smallest / len(cuts), top_value / len(cuts))
        gain = gain * jnp.repeat(jnp.exp(steps), shape[axis_at] // shards_of).reshape((-1,) + (1,) * (len(shape) - 1 - axis_at))
    return gain


def setup_inputs(seed: int = 0) -> dict:
    streams_of = jax.random.split(jax.random.key(seed), 7)
    volume = jnp.clip(jnp.exp(math.log(10.0) - 4.6051702 * jax.random.uniform(streams_of[0], (VOXELS,), jnp.float32) ** level_of(streams_of[0], (VOXELS,), ((0, 8),), -0.2, 0.2)), 0.1, 10.0)
    voxel_index = with_ends(jax.random.randint(streams_of[1], (ORIENTS, SLABS * ENTRIES), 0, VOX_DEV), jax.random.fold_in(streams_of[1], 1), 0, VOX_DEV - 1).astype(jnp.int32)
    pixel_index = with_ends(jax.random.randint(streams_of[2], (ORIENTS, SLABS * ENTRIES), 0, PIX), jax.random.fold_in(streams_of[2], 1), 0, PIX - 1).astype(jnp.int32)
    weights = jnp.clip(jnp.exp(math.log(0.5) - 2.306499 * jax.random.uniform(streams_of[3], (ORIENTS, SLABS * ENTRIES), jnp.float32) ** level_of(streams_of[3], (ORIENTS, SLABS * ENTRIES), ((0, 8),), -0.2, 0.2)), 0.049804688, 0.5).astype(jnp.bfloat16)
    background = jnp.clip(jnp.exp(jax.random.uniform(streams_of[4], (PIX,), jnp.float32, math.log(0.2), math.log(1.0))), 0.2, 1.0)
    counts = draw_counts(jax.random.fold_in(streams_of[6], 71), 0)
    return dict(volume=volume, voxel_index=voxel_index, pixel_index=pixel_index, weights=weights, background=background, counts=counts)


prior_weight = 0.05


def reference(volume, voxel_index, pixel_index, weights, background, counts):
    columns = jnp.arange(SLABS * ENTRIES, dtype=jnp.int32) // ENTRIES
    global_voxel = voxel_index + (columns * VOX_DEV)[None, :]
    values = volume[global_voxel]
    wfloat = weights.astype(jnp.float32)
    contrib = wfloat * values
    rows = jnp.arange(ORIENTS, dtype=jnp.int32)[:, None]
    slices = jnp.zeros((ORIENTS, PIX), jnp.float32).at[rows, pixel_index].add(contrib) + background[None, :]
    counts_f = counts.astype(jnp.float32)
    loglike = lax.dot_general(jnp.log(slices), counts_f, (((1,), (1,)), ((), ())), precision=lax.Precision.HIGHEST, preferred_element_type=jnp.float32)
    loglike = loglike - jnp.sum(slices, axis=1)[:, None]
    score = (64.0 / PIX) * loglike
    top = jnp.max(score, axis=0)
    expo_terms = jnp.exp(score - top[None, :])
    probs = expo_terms / jnp.sum(expo_terms, axis=0)[None, :]
    numerator = jnp.dot(probs, counts_f, precision=lax.Precision.HIGHEST, preferred_element_type=jnp.float32)
    denominator = jnp.sum(probs, axis=1)
    picked = jnp.take_along_axis(numerator, pixel_index, axis=1)
    entry_num = wfloat * picked
    entry_den = wfloat * denominator[:, None]
    acc_num = jnp.zeros((VOXELS,), jnp.float32).at[global_voxel].add(entry_num)
    acc_den = jnp.zeros((VOXELS,), jnp.float32).at[global_voxel].add(entry_den)
    new_volume = (acc_num + prior_weight * volume) / (acc_den + prior_weight)
    return new_volume, probs
```

```python
import functools

import jax
import jax.numpy as jnp
from jax import lax
from jax.experimental import pallas as pl
from jax.experimental.pallas import tpu as pltpu
from jax.sharding import PartitionSpec as P

prior_weight = 0.05
LANES = 128
GROUP = 16
CHUNKS = 4
MESH = pl.DeviceIdType.MESH
F32, BF16, I32 = jnp.float32, jnp.bfloat16, jnp.int32


def each(count, body):
    if count <= 16:
        for i in range(count):
            body(i)
    else:
        lax.fori_loop(0, count, lambda i, _: (body(i), 0)[1], 0)


def at(i, size):
    return pl.ds(i * size if isinstance(i, int) else pl.multiple_of(i * size, size), size)


def parts(x, count):
    out = []
    for _ in range(count):
        p = x.astype(BF16).astype(F32)
        out.append(p)
        x = x - p
    return out


def dot_nt(a, b):
    return lax.dot_general(a, b, (((1,), (1,)), ((), ())), preferred_element_type=F32)


def lane_pick(rows, lane):
    return jnp.take_along_axis(rows, lane, axis=1, mode="promise_in_bounds")


def kernel(
    n, m,
    vol_ref, vidx_ref, pix_ref, w_ref, bg_ref, cnt_ref,
    newv_ref, probs_ref,
    cnt_i, cnt_b, vals, got_vals, pw, got_pw, pix_hot, spread, logs, scores, all_scores,
    pix_mine, w_mine, row_hot, col_val, sums, acc_scr,
    cnt_sem, val_send, val_recv, pw_send, pw_recv, sc_send, sc_recv, sum_send, sum_recv,
):
    me = lax.axis_index("orient")
    fr = lax.axis_index("frame")
    local = pix_ref.shape[0]
    total = n * local
    frames, pixels = cnt_ref.shape
    pix_rows = pixels // LANES
    vox_rows = vol_ref.shape[0]
    step = frames // CHUNKS
    per_group = GROUP // local

    barrier = pltpu.get_barrier_semaphore()

    def greet_o(d):
        pl.semaphore_signal(barrier, inc=1, device_id={"orient": lax.rem(me + d + 1, n)}, device_id_type=MESH)

    def greet_f(d):
        pl.semaphore_signal(barrier, inc=1, device_id={"frame": lax.rem(fr + d + 1, m)}, device_id_type=MESH)

    each(n - 1, greet_o)
    each(m - 1, greet_f)

    loads = [
        pltpu.make_async_copy(
            cnt_ref.at[pl.ds(i * step, step)], cnt_i.at[pl.ds(i * step, step)], cnt_sem.at[i]
        )
        for i in range(CHUNKS)
    ]
    for c in loads:
        c.start()

    def gather_group(g):
        idx = vidx_ref[at(g, GROUP), :]
        row = lax.shift_right_logical(idx, 7)
        lane = lax.bitwise_and(idx, LANES - 1)

        def body(t, acc):
            base = pl.multiple_of(t * 8, 8)
            block = vol_ref[pl.ds(base, 8), :]
            for i in range(8):
                line = jnp.broadcast_to(block[i : i + 1, :], (GROUP, LANES))
                acc = jnp.where(row == base + i, lane_pick(line, lane), acc)
            return acc

        acc = lax.fori_loop(0, vox_rows // 8, body, jnp.zeros((GROUP, LANES), F32), unroll=2)
        for j in range(per_group):
            vals[g * per_group + j] = acc[j * local : (j + 1) * local, :]

    each(total // GROUP, gather_group)

    def fill_pw(j):
        pw[j, 0:local] = pix_ref[:, at(j, LANES)].astype(F32)
        pw[j, local : 2 * local] = w_ref[:, at(j, LANES)].astype(F32)

    each(n, fill_pw)

    pl.semaphore_wait(barrier, n + m - 2)

    def val_copy(d):
        to = lax.rem(me + d + 1, n)
        return pltpu.make_async_remote_copy(
            src_ref=vals.at[to], dst_ref=got_vals.at[me],
            send_sem=val_send.at[d], recv_sem=val_recv.at[me],
            device_id={"orient": to}, device_id_type=MESH,
        )

    def pw_copy(d):
        to = lax.rem(me + d + 1, n)
        return pltpu.make_async_remote_copy(
            src_ref=pw.at[to], dst_ref=got_pw.at[me],
            send_sem=pw_send.at[d], recv_sem=pw_recv.at[me],
            device_id={"orient": to}, device_id_type=MESH,
        )

    def score_copy(d):
        to = lax.rem(me + d + 1, n)
        return pltpu.make_async_remote_copy(
            src_ref=scores, dst_ref=all_scores.at[me],
            send_sem=sc_send.at[d], recv_sem=sc_recv.at[me],
            device_id={"orient": to}, device_id_type=MESH,
        )

    def sum_copy(d):
        to = lax.rem(fr + d + 1, m)
        return pltpu.make_async_remote_copy(
            src_ref=sums.at[fr], dst_ref=sums.at[fr],
            send_sem=sum_send.at[d], recv_sem=sum_recv.at[fr],
            device_id={"frame": to}, device_id_type=MESH,
        )

    def arrivals(buffer, sems, own, count, send_sems):
        def body(d):
            src = lax.rem(own + d + 1, count)
            pltpu.make_async_remote_copy(
                src_ref=buffer.at[src], dst_ref=buffer.at[src],
                send_sem=send_sems.at[d], recv_sem=sems.at[src],
                device_id={"orient": me}, device_id_type=MESH,
            ).wait_recv()

        each(count - 1, body)

    each(n - 1, lambda d: val_copy(d).start())
    each(n - 1, lambda d: pw_copy(d).start())
    got_vals[me] = vals[me]
    got_pw[me] = pw[me]

    def hot_pix(s):
        for o in range(local):
            lane = lax.bitwise_and(pix_ref[pl.ds(o, 1), at(s, LANES)], LANES - 1)
            hot = lax.broadcasted_iota(I32, (LANES, LANES), 0) == lane
            pix_hot[o, :, at(s, LANES)] = jnp.where(hot, 1.0, 0.0).astype(BF16)

    each(n, hot_pix)

    for i in range(CHUNKS):
        loads[i].wait()

        def cast(t, _, i=i):
            rows = pl.ds(pl.multiple_of(i * step + t * 16, 16), 16)
            cnt_b[rows, :] = cnt_i[rows, :].astype(F32).astype(BF16)
            return 0

        lax.fori_loop(0, step // 16, cast, 0)

    arrivals(got_vals, val_recv, me, n, val_send)

    def spread_slab(s):
        contrib = got_vals[s] * pw[s, local : 2 * local]
        for o in range(local):
            row = lax.shift_right_logical(pix_ref[pl.ds(o, 1), at(s, LANES)], 7)
            hit = lax.broadcasted_iota(I32, (pix_rows, LANES), 0) == row
            for k, part in enumerate(parts(contrib[o : o + 1, :], 3)):
                spread[o, k * pix_rows : (k + 1) * pix_rows, at(s, LANES)] = jnp.where(hit, part, 0.0).astype(BF16)

    each(n, spread_slab)

    logs[...] = jnp.zeros_like(logs)
    slice_sums = []
    for o in range(local):
        d3 = dot_nt(spread[o], pix_hot[o])
        sl = d3[0:pix_rows] + d3[pix_rows : 2 * pix_rows] + d3[2 * pix_rows : 3 * pix_rows] + bg_ref[...]
        slice_sums.append(jnp.sum(jnp.sum(sl, axis=1, keepdims=True), axis=0, keepdims=True))
        lg = jnp.log(sl)
        for r in range(pix_rows):
            logs[o : o + 1, r * LANES : (r + 1) * LANES] = lg[r : r + 1, :]
    pad = logs.shape[0]
    lv = logs[...]
    stack = jnp.concatenate(parts(lv, 3) + [jnp.zeros_like(lv)], axis=0).astype(BF16)
    ll = dot_nt(stack, cnt_b[...])
    ll = ll[0:pad] + ll[pad : 2 * pad] + ll[2 * pad : 3 * pad]
    scores[...] = (64.0 / pixels) * (ll[0:local] - jnp.concatenate(slice_sums, axis=0))
    each(n - 1, lambda d: score_copy(d).start())
    all_scores[me] = scores[...]

    arrivals(got_pw, pw_recv, me, n, pw_send)

    def unpack(g):
        for j in range(per_group):
            src = got_pw[g * per_group + j]
            pix_mine[g, j * local : (j + 1) * local] = src[0:local].astype(I32)
            w_mine[g, j * local : (j + 1) * local] = src[local : 2 * local]

    each(total // GROUP, unpack)

    def hot_rows(g):
        idx = vidx_ref[at(g, GROUP), :]
        for o in range(GROUP):
            row = lax.shift_right_logical(idx[o : o + 1, :], 7)
            hit = lax.broadcasted_iota(I32, (vox_rows, LANES), 0) == row
            row_hot[:, o * LANES : (o + 1) * LANES] = jnp.where(hit, 1.0, 0.0).astype(BF16)

    hot_rows(0)

    arrivals(all_scores, sc_recv, me, n, sc_send)
    top = jnp.max(jnp.max(all_scores[...], axis=0), axis=0, keepdims=True)
    whole_sum = jnp.sum(jnp.sum(jnp.exp(all_scores[...] - top[None]), axis=0), axis=0, keepdims=True)
    probs_ref[...] = jnp.exp(scores[...] - top) / whole_sum

    def numerators(g):
        pieces = [
            jnp.exp(all_scores[g * per_group + j] - top) / whole_sum for j in range(per_group)
        ]
        pr = jnp.concatenate(pieces, axis=0)
        den = jnp.sum(pr, axis=1, keepdims=True)
        two = jnp.concatenate(parts(pr, 2), axis=0).astype(BF16)
        pix = pix_mine[g]
        row = lax.shift_right_logical(pix, 7)
        lane = lax.bitwise_and(pix, LANES - 1)
        acc = jnp.zeros((GROUP, LANES), F32)
        wide = 4
        for q in range(pix_rows // wide):
            d2 = jnp.dot(
                two, cnt_b[:, q * wide * LANES : (q + 1) * wide * LANES], preferred_element_type=F32
            )
            num = d2[0:GROUP] + d2[GROUP : 2 * GROUP]
            for i in range(wide):
                got = lane_pick(num[:, i * LANES : (i + 1) * LANES], lane)
                acc = jnp.where(row == q * wide + i, got, acc)
        sums[fr, 0, g] = acc
        sums[fr, 1, g] = jnp.broadcast_to(den, (GROUP, LANES))

    each(total // GROUP, numerators)
    each(m - 1, lambda d: sum_copy(d).start())

    def sum_arrivals(d):
        src = lax.rem(fr + d + 1, m)
        pltpu.make_async_remote_copy(
            src_ref=sums.at[src], dst_ref=sums.at[src],
            send_sem=sum_send.at[d], recv_sem=sum_recv.at[src],
            device_id={"frame": fr}, device_id_type=MESH,
        ).wait_recv()

    each(m - 1, sum_arrivals)

    def scatter(g):
        num, den = sums[0, 0, g], sums[0, 1, g]
        for f in range(1, m):
            num = num + sums[f, 0, g]
            den = den + sums[f, 1, g]
        wf = w_mine[g]
        four = parts(num * wf, 2) + parts(den * wf, 2)
        idx = vidx_ref[at(g, GROUP), :]
        lane = lax.bitwise_and(idx, LANES - 1)
        for o in range(GROUP):
            hit = lax.broadcasted_iota(I32, (LANES, LANES), 0) == lane[o : o + 1, :]
            for k in range(4):
                col_val[k * LANES : (k + 1) * LANES, o * LANES : (o + 1) * LANES] = jnp.where(
                    hit, four[k][o : o + 1, :], 0.0
                ).astype(BF16)
        return dot_nt(row_hot[...], col_val[...])

    def finish(acc):
        num = acc[:, 0:LANES] + acc[:, LANES : 2 * LANES]
        den = acc[:, 2 * LANES : 3 * LANES] + acc[:, 3 * LANES : 4 * LANES]
        newv_ref[...] = (num + prior_weight * vol_ref[...]) / (den + prior_weight)

    if total == GROUP:
        finish(scatter(0))
    else:
        acc_scr[...] = scatter(0)

        def more(g, _):
            hot_rows(g)
            acc_scr[...] += scatter(g)
            return 0

        lax.fori_loop(1, total // GROUP, more, 0)
        finish(acc_scr[...])

    each(n - 1, lambda d: val_copy(d).wait_send())
    each(n - 1, lambda d: pw_copy(d).wait_send())
    each(n - 1, lambda d: score_copy(d).wait_send())
    each(m - 1, lambda d: sum_copy(d).wait_send())


def on_device(n, m, volume, voxel_index, pixel_index, weights, background, counts):
    local, columns = pixel_index.shape
    total, entries = voxel_index.shape
    frames, pixels = counts.shape
    pix_rows = pixels // LANES
    vox_rows = volume.shape[0] // LANES
    groups = total // GROUP
    vmem = pl.BlockSpec(memory_space=pltpu.VMEM)
    dma = pltpu.SemaphoreType.DMA
    new_volume, probs = pl.pallas_call(
        functools.partial(kernel, n, m),
        out_shape=(
            jax.ShapeDtypeStruct((vox_rows, LANES), F32),
            jax.ShapeDtypeStruct((local, frames), F32),
        ),
        in_specs=[vmem] * 5 + [pl.BlockSpec(memory_space=pl.ANY)],
        out_specs=(vmem, vmem),
        scratch_shapes=[
            pltpu.VMEM((frames, pixels), I32),
            pltpu.VMEM((frames, pixels), BF16),
            pltpu.VMEM((n, local, LANES), F32),
            pltpu.VMEM((n, local, LANES), F32),
            pltpu.VMEM((n, 2 * local, LANES), F32),
            pltpu.VMEM((n, 2 * local, LANES), F32),
            pltpu.VMEM((local, LANES, columns), BF16),
            pltpu.VMEM((local, 3 * pix_rows, columns), BF16),
            pltpu.VMEM((8, pixels), F32),
            pltpu.VMEM((local, frames), F32),
            pltpu.VMEM((n, local, frames), F32),
            pltpu.VMEM((groups, GROUP, LANES), I32),
            pltpu.VMEM((groups, GROUP, LANES), F32),
            pltpu.VMEM((vox_rows, GROUP * LANES), BF16),
            pltpu.VMEM((4 * LANES, GROUP * LANES), BF16),
            pltpu.VMEM((m, 2, groups, GROUP, LANES), F32),
            pltpu.VMEM((vox_rows if groups > 1 else 8, 4 * LANES), F32),
            dma((CHUNKS,)),
            dma((n,)), dma((n,)), dma((n,)), dma((n,)), dma((n,)), dma((n,)),
            dma((m,)), dma((m,)),
        ],
        compiler_params=pltpu.CompilerParams(
            collective_id=0, has_side_effects=True, vmem_limit_bytes=44 * 1024 * 1024
        ),
    )(
        volume.reshape(vox_rows, LANES), voxel_index, pixel_index, weights,
        background.reshape(pix_rows, LANES), counts,
    )
    return (new_volume.reshape(-1), probs)


def solution(mesh):
    n, m = mesh.shape["orient"], mesh.shape["frame"]
    in_specs = (
        P("orient"),
        P(None, "orient"),
        P("orient", None),
        P("orient", None),
        P(),
        P("frame", None),
    )
    out_specs = (P("orient"), P("orient", "frame"))
    return jax.shard_map(
        functools.partial(on_device, n, m), mesh=mesh, in_specs=in_specs, out_specs=out_specs, check_vma=False
    )
```

```python
import functools

import jax
import jax.numpy as jnp
from jax import lax
from jax.experimental import pallas as pl
from jax.experimental.pallas import tpu as pltpu
from jax.sharding import PartitionSpec as P

prior_weight = 0.05
LANES = 128
VMEM_ALL = 64 * 1024 * 1024
LEFT = 256 * 1024
GROUP = 16
CHUNKS = 4
MESH = pl.DeviceIdType.MESH
F32, BF16, I32 = jnp.float32, jnp.bfloat16, jnp.int32


def each(count, body):
    if count <= 16:
        for i in range(count):
            body(i)
    else:
        lax.fori_loop(0, count, lambda i, _: (body(i), 0)[1], 0)


def at(i, size):
    return pl.ds(i * size if isinstance(i, int) else pl.multiple_of(i * size, size), size)


def parts(x, count):
    out = []
    for _ in range(count):
        p = x.astype(BF16).astype(F32)
        out.append(p)
        x = x - p
    return out


def dot_nt(a, b):
    return lax.dot_general(a, b, (((1,), (1,)), ((), ())), preferred_element_type=F32)


def lane_pick(rows, lane):
    return jnp.take_along_axis(rows, lane, axis=1, mode="promise_in_bounds")


def kernel(
    n, m,
    vol_hbm, vidx_hbm, pix_hbm, w_hbm, bg_hbm, cnt_ref,
    newv_ref, probs_ref,
    vol_ref, vidx_ref, pix_ref, w_ref, bg_ref,
    cnt_i, cnt_b, vals, got_vals, pw, got_pw, pix_hot, spread, logs, scores, all_scores,
    pix_mine, w_mine, row_hot, col_val, sums, acc_scr,
    in_sem, cnt_sem, val_send, val_recv, pw_send, pw_recv, sc_send, sc_recv, sum_send, sum_recv,
):
    me = lax.axis_index("orient")
    fr = lax.axis_index("frame")
    local = pix_hbm.shape[0]
    total = n * local
    frames, pixels = cnt_ref.shape
    pix_rows = pixels // LANES
    vox_rows = vol_ref.shape[0]
    step = frames // CHUNKS
    per_group = GROUP // local

    barrier = pltpu.get_barrier_semaphore()

    def greet_o(d):
        pl.semaphore_signal(barrier, inc=1, device_id={"orient": lax.rem(me + d + 1, n)}, device_id_type=MESH)

    def greet_f(d):
        pl.semaphore_signal(barrier, inc=1, device_id={"frame": lax.rem(fr + d + 1, m)}, device_id_type=MESH)

    small = [
        pltpu.make_async_copy(src, dst, in_sem.at[i])
        for i, (src, dst) in enumerate(
            [
                (vidx_hbm, vidx_ref), (vol_hbm, vol_ref), (pix_hbm, pix_ref),
                (w_hbm, w_ref), (bg_hbm, bg_ref),
            ]
        )
    ]
    each(n - 1, greet_o)
    each(m - 1, greet_f)
    for c in small:
        c.start()

    loads = [
        pltpu.make_async_copy(
            cnt_ref.at[pl.ds(i * step, step)], cnt_i.at[pl.ds(i * step, step)], cnt_sem.at[i]
        )
        for i in range(CHUNKS)
    ]
    for c in loads:
        c.start()
    for c in small:
        c.wait()

    def gather_group(g):
        idx = vidx_ref[at(g, GROUP), :]
        row = lax.shift_right_logical(idx, 7)
        lane = lax.bitwise_and(idx, LANES - 1)

        def body(t, acc):
            base = pl.multiple_of(t * 8, 8)
            block = vol_ref[pl.ds(base, 8), :]
            for i in range(8):
                line = jnp.broadcast_to(block[i : i + 1, :], (GROUP, LANES))
                acc = jnp.where(row == base + i, lane_pick(line, lane), acc)
            return acc

        acc = lax.fori_loop(0, vox_rows // 8, body, jnp.zeros((GROUP, LANES), F32), unroll=2)
        for j in range(per_group):
            vals[g * per_group + j] = acc[j * local : (j + 1) * local, :]

    each(total // GROUP, gather_group)

    def fill_pw(j):
        pw[j, 0:local] = pix_ref[:, at(j, LANES)].astype(F32)
        pw[j, local : 2 * local] = w_ref[:, at(j, LANES)].astype(F32)

    each(n, fill_pw)

    pl.semaphore_wait(barrier, n + m - 2)

    def val_copy(d):
        to = lax.rem(me + d + 1, n)
        return pltpu.make_async_remote_copy(
            src_ref=vals.at[to], dst_ref=got_vals.at[me],
            send_sem=val_send.at[d], recv_sem=val_recv.at[me],
            device_id={"orient": to}, device_id_type=MESH,
        )

    def pw_copy(d):
        to = lax.rem(me + d + 1, n)
        return pltpu.make_async_remote_copy(
            src_ref=pw.at[to], dst_ref=got_pw.at[me],
            send_sem=pw_send.at[d], recv_sem=pw_recv.at[me],
            device_id={"orient": to}, device_id_type=MESH,
        )

    def score_copy(d):
        to = lax.rem(me + d + 1, n)
        return pltpu.make_async_remote_copy(
            src_ref=scores, dst_ref=all_scores.at[me],
            send_sem=sc_send.at[d], recv_sem=sc_recv.at[me],
            device_id={"orient": to}, device_id_type=MESH,
        )

    def sum_copy(d):
        to = lax.rem(fr + d + 1, m)
        return pltpu.make_async_remote_copy(
            src_ref=sums.at[fr], dst_ref=sums.at[fr],
            send_sem=sum_send.at[d], recv_sem=sum_recv.at[fr],
            device_id={"frame": to}, device_id_type=MESH,
        )

    def arrivals(buffer, sems, own, count, send_sems):
        def body(d):
            src = lax.rem(own + d + 1, count)
            pltpu.make_async_remote_copy(
                src_ref=buffer.at[src], dst_ref=buffer.at[src],
                send_sem=send_sems.at[d], recv_sem=sems.at[src],
                device_id={"orient": me}, device_id_type=MESH,
            ).wait_recv()

        each(count - 1, body)

    each(n - 1, lambda d: val_copy(d).start())
    each(n - 1, lambda d: pw_copy(d).start())
    got_vals[me] = vals[me]
    got_pw[me] = pw[me]

    def hot_pix(s):
        for o in range(local):
            lane = lax.bitwise_and(pix_ref[pl.ds(o, 1), at(s, LANES)], LANES - 1)
            hot = lax.broadcasted_iota(I32, (LANES, LANES), 0) == lane
            pix_hot[o, :, at(s, LANES)] = jnp.where(hot, 1.0, 0.0).astype(BF16)

    each(n, hot_pix)

    for i in range(CHUNKS):
        loads[i].wait()

        def cast(t, _, i=i):
            rows = pl.ds(pl.multiple_of(i * step + t * 16, 16), 16)
            cnt_b[rows, :] = cnt_i[rows, :].astype(F32).astype(BF16)
            return 0

        lax.fori_loop(0, step // 16, cast, 0)

    arrivals(got_vals, val_recv, me, n, val_send)

    def spread_slab(s):
        contrib = got_vals[s] * pw[s, local : 2 * local]
        for o in range(local):
            row = lax.shift_right_logical(pix_ref[pl.ds(o, 1), at(s, LANES)], 7)
            hit = lax.broadcasted_iota(I32, (pix_rows, LANES), 0) == row
            for k, part in enumerate(parts(contrib[o : o + 1, :], 3)):
                spread[o, k * pix_rows : (k + 1) * pix_rows, at(s, LANES)] = jnp.where(hit, part, 0.0).astype(BF16)

    each(n, spread_slab)

    logs[...] = jnp.zeros_like(logs)
    slice_sums = []
    for o in range(local):
        d3 = dot_nt(spread[o], pix_hot[o])
        sl = d3[0:pix_rows] + d3[pix_rows : 2 * pix_rows] + d3[2 * pix_rows : 3 * pix_rows] + bg_ref[...]
        slice_sums.append(jnp.sum(jnp.sum(sl, axis=1, keepdims=True), axis=0, keepdims=True))
        lg = jnp.log(sl)
        for r in range(pix_rows):
            logs[o : o + 1, r * LANES : (r + 1) * LANES] = lg[r : r + 1, :]
    pad = logs.shape[0]
    lv = logs[...]
    stack = jnp.concatenate(parts(lv, 3) + [jnp.zeros_like(lv)], axis=0).astype(BF16)
    ll = dot_nt(stack, cnt_b[...])
    ll = ll[0:pad] + ll[pad : 2 * pad] + ll[2 * pad : 3 * pad]
    scores[...] = (64.0 / pixels) * (ll[0:local] - jnp.concatenate(slice_sums, axis=0))
    each(n - 1, lambda d: score_copy(d).start())
    all_scores[me] = scores[...]

    arrivals(got_pw, pw_recv, me, n, pw_send)

    def unpack(g):
        for j in range(per_group):
            src = got_pw[g * per_group + j]
            pix_mine[g, j * local : (j + 1) * local] = src[0:local].astype(I32)
            w_mine[g, j * local : (j + 1) * local] = src[local : 2 * local]

    each(total // GROUP, unpack)

    def hot_rows(g):
        idx = vidx_ref[at(g, GROUP), :]
        for o in range(GROUP):
            row = lax.shift_right_logical(idx[o : o + 1, :], 7)
            hit = lax.broadcasted_iota(I32, (vox_rows, LANES), 0) == row
            row_hot[:, o * LANES : (o + 1) * LANES] = jnp.where(hit, 1.0, 0.0).astype(BF16)

    hot_rows(0)

    arrivals(all_scores, sc_recv, me, n, sc_send)
    top = jnp.max(jnp.max(all_scores[...], axis=0), axis=0, keepdims=True)
    whole_sum = jnp.sum(jnp.sum(jnp.exp(all_scores[...] - top[None]), axis=0), axis=0, keepdims=True)
    probs_ref[...] = jnp.exp(scores[...] - top) / whole_sum

    def numerators(g):
        pieces = [
            jnp.exp(all_scores[g * per_group + j] - top) / whole_sum for j in range(per_group)
        ]
        pr = jnp.concatenate(pieces, axis=0)
        den = jnp.sum(pr, axis=1, keepdims=True)
        two = jnp.concatenate(parts(pr, 2), axis=0).astype(BF16)
        pix = pix_mine[g]
        row = lax.shift_right_logical(pix, 7)
        lane = lax.bitwise_and(pix, LANES - 1)
        acc = jnp.zeros((GROUP, LANES), F32)
        wide = 4
        for q in range(pix_rows // wide):
            d2 = jnp.dot(
                two, cnt_b[:, q * wide * LANES : (q + 1) * wide * LANES], preferred_element_type=F32
            )
            num = d2[0:GROUP] + d2[GROUP : 2 * GROUP]
            for i in range(wide):
                got = lane_pick(num[:, i * LANES : (i + 1) * LANES], lane)
                acc = jnp.where(row == q * wide + i, got, acc)
        sums[fr, 0, g] = acc
        sums[fr, 1, g] = jnp.broadcast_to(den, (GROUP, LANES))

    each(total // GROUP, numerators)
    each(m - 1, lambda d: sum_copy(d).start())

    def sum_arrivals(d):
        src = lax.rem(fr + d + 1, m)
        pltpu.make_async_remote_copy(
            src_ref=sums.at[src], dst_ref=sums.at[src],
            send_sem=sum_send.at[d], recv_sem=sum_recv.at[src],
            device_id={"frame": fr}, device_id_type=MESH,
        ).wait_recv()

    each(m - 1, sum_arrivals)

    def scatter(g):
        num, den = sums[0, 0, g], sums[0, 1, g]
        for f in range(1, m):
            num = num + sums[f, 0, g]
            den = den + sums[f, 1, g]
        wf = w_mine[g]
        four = parts(num * wf, 2) + parts(den * wf, 2)
        idx = vidx_ref[at(g, GROUP), :]
        lane = lax.bitwise_and(idx, LANES - 1)
        for o in range(GROUP):
            hit = lax.broadcasted_iota(I32, (LANES, LANES), 0) == lane[o : o + 1, :]
            for k in range(4):
                col_val[k * LANES : (k + 1) * LANES, o * LANES : (o + 1) * LANES] = jnp.where(
                    hit, four[k][o : o + 1, :], 0.0
                ).astype(BF16)
        return dot_nt(row_hot[...], col_val[...])

    def finish(acc):
        num = acc[:, 0:LANES] + acc[:, LANES : 2 * LANES]
        den = acc[:, 2 * LANES : 3 * LANES] + acc[:, 3 * LANES : 4 * LANES]
        newv_ref[...] = (num + prior_weight * vol_ref[...]) / (den + prior_weight)

    if total == GROUP:
        finish(scatter(0))
    else:
        acc_scr[...] = scatter(0)

        def more(g, _):
            hot_rows(g)
            acc_scr[...] += scatter(g)
            return 0

        lax.fori_loop(1, total // GROUP, more, 0)
        finish(acc_scr[...])

    each(n - 1, lambda d: val_copy(d).wait_send())
    each(n - 1, lambda d: pw_copy(d).wait_send())
    each(n - 1, lambda d: score_copy(d).wait_send())
    each(m - 1, lambda d: sum_copy(d).wait_send())


def hand_out(vol_ref, probs_ref, vol_out, probs_out, sem):
    copies = [
        pltpu.make_async_copy(vol_ref, vol_out, sem.at[0]),
        pltpu.make_async_copy(probs_ref, probs_out, sem.at[1]),
    ]
    for c in copies:
        c.start()
    for c in copies:
        c.wait()


def on_device(n, m, volume, voxel_index, pixel_index, weights, background, counts):
    local, columns = pixel_index.shape
    total, entries = voxel_index.shape
    frames, pixels = counts.shape
    pix_rows = pixels // LANES
    vox_rows = volume.shape[0] // LANES
    groups = total // GROUP
    vmem = pl.BlockSpec(memory_space=pltpu.VMEM)
    hbm = pl.BlockSpec(memory_space=pltpu.MemorySpace.HBM)
    dma = pltpu.SemaphoreType.DMA
    new_volume, probs = pl.pallas_call(
        functools.partial(kernel, n, m),
        out_shape=(
            pltpu.VMEM((vox_rows, LANES), F32),
            pltpu.VMEM((local, frames), F32),
        ),
        in_specs=[hbm] * 6,
        out_specs=(vmem, vmem),
        scratch_shapes=[
            pltpu.VMEM((vox_rows, LANES), F32),
            pltpu.VMEM((total, entries), I32),
            pltpu.VMEM((local, columns), I32),
            pltpu.VMEM((local, columns), BF16),
            pltpu.VMEM((pix_rows, LANES), F32),
            pltpu.VMEM((frames, pixels), I32),
            pltpu.VMEM((frames, pixels), BF16),
            pltpu.VMEM((n, local, LANES), F32),
            pltpu.VMEM((n, local, LANES), F32),
            pltpu.VMEM((n, 2 * local, LANES), F32),
            pltpu.VMEM((n, 2 * local, LANES), F32),
            pltpu.VMEM((local, LANES, columns), BF16),
            pltpu.VMEM((local, 3 * pix_rows, columns), BF16),
            pltpu.VMEM((8, pixels), F32),
            pltpu.VMEM((local, frames), F32),
            pltpu.VMEM((n, local, frames), F32),
            pltpu.VMEM((groups, GROUP, LANES), I32),
            pltpu.VMEM((groups, GROUP, LANES), F32),
            pltpu.VMEM((vox_rows, GROUP * LANES), BF16),
            pltpu.VMEM((4 * LANES, GROUP * LANES), BF16),
            pltpu.VMEM((m, 2, groups, GROUP, LANES), F32),
            pltpu.VMEM((vox_rows if groups > 1 else 8, 4 * LANES), F32),
            dma((5,)), dma((CHUNKS,)),
            dma((n,)), dma((n,)), dma((n,)), dma((n,)), dma((n,)), dma((n,)),
            dma((m,)), dma((m,)),
        ],
        compiler_params=pltpu.CompilerParams(
            collective_id=0, has_side_effects=True, vmem_limit_bytes=VMEM_ALL - 4 * (vox_rows * LANES + local * frames) - LEFT
        ),
    )(
        volume.reshape(vox_rows, LANES), voxel_index, pixel_index, weights,
        background.reshape(pix_rows, LANES), counts,
    )
    new_volume, probs = pl.pallas_call(
        hand_out,
        out_shape=(
            jax.ShapeDtypeStruct(new_volume.shape, F32),
            jax.ShapeDtypeStruct(probs.shape, F32),
        ),
        in_specs=[vmem] * 2,
        out_specs=[pl.BlockSpec(memory_space=pl.ANY)] * 2,
        scratch_shapes=[dma((2,))],
    )(new_volume, probs)
    return (new_volume.reshape(-1), probs)


def solution(mesh):
    n, m = mesh.shape["orient"], mesh.shape["frame"]
    in_specs = (
        P("orient"),
        P(None, "orient"),
        P("orient", None),
        P("orient", None),
        P(),
        P("frame", None),
    )
    out_specs = (P("orient"), P("orient", "frame"))
    return jax.shard_map(
        functools.partial(on_device, n, m), mesh=mesh, in_specs=in_specs, out_specs=out_specs, check_vma=False
    )
```

```python
import functools

import jax
import jax.numpy as jnp
from jax import lax
from jax.experimental import pallas as pl
from jax.experimental.pallas import tpu as pltpu
from jax.sharding import PartitionSpec as P

prior_weight = 0.05
LANES = 128
VMEM_ALL = 64 * 1024 * 1024
LEFT = 256 * 1024
GROUP = 16
CHUNKS = 4
MESH = pl.DeviceIdType.MESH
F32, BF16, I32 = jnp.float32, jnp.bfloat16, jnp.int32


def each(count, body):
    if count <= 16:
        for i in range(count):
            body(i)
    else:
        lax.fori_loop(0, count, lambda i, _: (body(i), 0)[1], 0)


def at(i, size):
    return pl.ds(i * size if isinstance(i, int) else pl.multiple_of(i * size, size), size)


def parts(x, count):
    out = []
    for _ in range(count):
        p = x.astype(BF16).astype(F32)
        out.append(p)
        x = x - p
    return out


def dot_nt(a, b):
    return lax.dot_general(a, b, (((1,), (1,)), ((), ())), preferred_element_type=F32)


def lane_pick(rows, lane):
    return jnp.take_along_axis(rows, lane, axis=1, mode="promise_in_bounds")


def kernel(
    n, m,
    vol_hbm, vidx_hbm, pix_hbm, w_hbm, bg_hbm, cnt_ref,
    newv_ref, probs_ref,
    vol_ref, vidx_ref, pix_ref, w_ref, bg_ref,
    cnt_i, cnt_b, vals, got_vals, pw, got_pw, pix_hot, spread, logs, scores, all_scores,
    pix_mine, w_mine, row_hot, col_val, sums, acc_scr,
    in_sem, cnt_sem, val_send, val_recv, pw_send, pw_recv, sc_send, sc_recv, sum_send, sum_recv,
):
    me = lax.axis_index("orient")
    fr = lax.axis_index("frame")
    local = pix_hbm.shape[0]
    total = n * local
    frames, pixels = cnt_ref.shape
    pix_rows = pixels // LANES
    vox_rows = vol_ref.shape[0]
    step = frames // CHUNKS
    per_group = GROUP // local

    barrier = pltpu.get_barrier_semaphore()

    def greet_o(d):
        pl.semaphore_signal(barrier, inc=1, device_id={"orient": lax.rem(me + d + 1, n)}, device_id_type=MESH)

    def greet_f(d):
        pl.semaphore_signal(barrier, inc=1, device_id={"frame": lax.rem(fr + d + 1, m)}, device_id_type=MESH)

    small = [
        pltpu.make_async_copy(src, dst, in_sem.at[i])
        for i, (src, dst) in enumerate(
            [
                (vidx_hbm, vidx_ref), (vol_hbm, vol_ref), (pix_hbm, pix_ref),
                (w_hbm, w_ref), (bg_hbm, bg_ref),
            ]
        )
    ]
    each(n - 1, greet_o)
    each(m - 1, greet_f)
    for c in small:
        c.start()

    loads = [
        pltpu.make_async_copy(
            cnt_ref.at[pl.ds(i * step, step)], cnt_i.at[pl.ds(i * step, step)], cnt_sem.at[i]
        )
        for i in range(CHUNKS)
    ]
    for c in loads:
        c.start()
    for c in small:
        c.wait()

    def gather_group(g):
        idx = vidx_ref[at(g, GROUP), :]
        row = lax.shift_right_logical(idx, 7)
        lane = lax.bitwise_and(idx, LANES - 1)

        def body(t, acc):
            base = pl.multiple_of(t * 8, 8)
            block = vol_ref[pl.ds(base, 8), :]
            for i in range(8):
                line = jnp.broadcast_to(block[i : i + 1, :], (GROUP, LANES))
                acc = jnp.where(row == base + i, lane_pick(line, lane), acc)
            return acc

        acc = lax.fori_loop(0, vox_rows // 8, body, jnp.zeros((GROUP, LANES), F32), unroll=2)
        for j in range(per_group):
            vals[g * per_group + j] = acc[j * local : (j + 1) * local, :]

    each(total // GROUP, gather_group)

    def fill_pw(j):
        pw[j, 0:local] = pix_ref[:, at(j, LANES)].astype(F32)
        pw[j, local : 2 * local] = w_ref[:, at(j, LANES)].astype(F32)

    each(n, fill_pw)

    pl.semaphore_wait(barrier, n + m - 2)

    def val_copy(d):
        to = lax.rem(me + d + 1, n)
        return pltpu.make_async_remote_copy(
            src_ref=vals.at[to], dst_ref=got_vals.at[me],
            send_sem=val_send.at[d], recv_sem=val_recv.at[me],
            device_id={"orient": to}, device_id_type=MESH,
        )

    def pw_copy(d):
        to = lax.rem(me + d + 1, n)
        return pltpu.make_async_remote_copy(
            src_ref=pw.at[to], dst_ref=got_pw.at[me],
            send_sem=pw_send.at[d], recv_sem=pw_recv.at[me],
            device_id={"orient": to}, device_id_type=MESH,
        )

    def score_copy(d):
        to = lax.rem(me + d + 1, n)
        return pltpu.make_async_remote_copy(
            src_ref=scores, dst_ref=all_scores.at[me],
            send_sem=sc_send.at[d], recv_sem=sc_recv.at[me],
            device_id={"orient": to}, device_id_type=MESH,
        )

    def sum_copy(d):
        to = lax.rem(fr + d + 1, m)
        return pltpu.make_async_remote_copy(
            src_ref=sums.at[fr], dst_ref=sums.at[fr],
            send_sem=sum_send.at[d], recv_sem=sum_recv.at[fr],
            device_id={"frame": to}, device_id_type=MESH,
        )

    def arrivals(buffer, sems, own, count, send_sems):
        def body(d):
            src = lax.rem(own + d + 1, count)
            pltpu.make_async_remote_copy(
                src_ref=buffer.at[src], dst_ref=buffer.at[src],
                send_sem=send_sems.at[d], recv_sem=sems.at[src],
                device_id={"orient": me}, device_id_type=MESH,
            ).wait_recv()

        each(count - 1, body)

    each(n - 1, lambda d: val_copy(d).start())
    each(n - 1, lambda d: pw_copy(d).start())
    got_vals[me] = vals[me]
    got_pw[me] = pw[me]

    def hot_pix(s):
        for o in range(local):
            lane = lax.bitwise_and(pix_ref[pl.ds(o, 1), at(s, LANES)], LANES - 1)
            hot = lax.broadcasted_iota(I32, (LANES, LANES), 0) == lane
            pix_hot[o, :, at(s, LANES)] = jnp.where(hot, 1.0, 0.0).astype(BF16)

    each(n, hot_pix)

    for i in range(CHUNKS):
        loads[i].wait()

        def cast(t, _, i=i):
            rows = pl.ds(pl.multiple_of(i * step + t * 16, 16), 16)
            cnt_b[rows, :] = cnt_i[rows, :].astype(F32).astype(BF16)
            return 0

        lax.fori_loop(0, step // 16, cast, 0)

    arrivals(got_vals, val_recv, me, n, val_send)

    def spread_slab(s):
        contrib = got_vals[s] * pw[s, local : 2 * local]
        for o in range(local):
            row = lax.shift_right_logical(pix_ref[pl.ds(o, 1), at(s, LANES)], 7)
            hit = lax.broadcasted_iota(I32, (pix_rows, LANES), 0) == row
            for k, part in enumerate(parts(contrib[o : o + 1, :], 3)):
                spread[o, k * pix_rows : (k + 1) * pix_rows, at(s, LANES)] = jnp.where(hit, part, 0.0).astype(BF16)

    each(n, spread_slab)

    logs[...] = jnp.zeros_like(logs)
    slice_sums = []
    for o in range(local):
        d3 = dot_nt(spread[o], pix_hot[o])
        sl = d3[0:pix_rows] + d3[pix_rows : 2 * pix_rows] + d3[2 * pix_rows : 3 * pix_rows] + bg_ref[...]
        slice_sums.append(jnp.sum(jnp.sum(sl, axis=1, keepdims=True), axis=0, keepdims=True))
        lg = jnp.log(sl)
        for r in range(pix_rows):
            logs[o : o + 1, r * LANES : (r + 1) * LANES] = lg[r : r + 1, :]
    pad = logs.shape[0]
    lv = logs[...]
    stack = jnp.concatenate(parts(lv, 3) + [jnp.zeros_like(lv)], axis=0).astype(BF16)
    ll = jnp.transpose(dot_nt(cnt_b[...], stack))
    ll = ll[0:pad] + ll[pad : 2 * pad] + ll[2 * pad : 3 * pad]
    scores[...] = (64.0 / pixels) * (ll[0:local] - jnp.concatenate(slice_sums, axis=0))
    each(n - 1, lambda d: score_copy(d).start())
    all_scores[me] = scores[...]

    arrivals(got_pw, pw_recv, me, n, pw_send)

    def unpack(g):
        for j in range(per_group):
            src = got_pw[g * per_group + j]
            pix_mine[g, j * local : (j + 1) * local] = src[0:local].astype(I32)
            w_mine[g, j * local : (j + 1) * local] = src[local : 2 * local]

    each(total // GROUP, unpack)

    def hot_rows(g):
        idx = vidx_ref[at(g, GROUP), :]
        for o in range(GROUP):
            row = lax.shift_right_logical(idx[o : o + 1, :], 7)
            hit = lax.broadcasted_iota(I32, (vox_rows, LANES), 0) == row
            row_hot[:, o * LANES : (o + 1) * LANES] = jnp.where(hit, 1.0, 0.0).astype(BF16)

    hot_rows(0)

    arrivals(all_scores, sc_recv, me, n, sc_send)
    top = jnp.max(jnp.max(all_scores[...], axis=0), axis=0, keepdims=True)
    whole_sum = jnp.sum(jnp.sum(jnp.exp(all_scores[...] - top[None]), axis=0), axis=0, keepdims=True)

    own_lane = lax.broadcasted_iota(I32, (GROUP, LANES), 0) == lax.broadcasted_iota(I32, (GROUP, LANES), 1)

    def numerators(g):
        pieces = [
            jnp.exp(all_scores[g * per_group + j] - top) / whole_sum for j in range(per_group)
        ]
        pr = jnp.concatenate(pieces, axis=0)
        den = jnp.sum(pr, axis=1, keepdims=True)
        two = jnp.concatenate(parts(pr, 2), axis=0).astype(BF16)
        pix = pix_mine[g]
        row = lax.shift_right_logical(pix, 7)
        lane = lax.bitwise_and(pix, LANES - 1)
        acc = jnp.zeros((GROUP, LANES), F32)
        wide = 4
        for q in range(pix_rows // wide):
            d2 = jnp.dot(
                two, cnt_b[:, q * wide * LANES : (q + 1) * wide * LANES], preferred_element_type=F32
            )
            num = d2[0:GROUP] + d2[GROUP : 2 * GROUP]
            for i in range(wide):
                got = lane_pick(num[:, i * LANES : (i + 1) * LANES], lane)
                acc = jnp.where(row == q * wide + i, got, acc)
        sums[fr, g, 0:GROUP] = acc
        sums[fr, g, GROUP:] = jnp.broadcast_to(
            jnp.sum(jnp.where(own_lane, den, 0.0), axis=0, keepdims=True), (8, LANES)
        )

    each(total // GROUP, numerators)
    each(m - 1, lambda d: sum_copy(d).start())
    probs_ref[...] = jnp.exp(scores[...] - top) / whole_sum

    def sum_arrivals(d):
        src = lax.rem(fr + d + 1, m)
        pltpu.make_async_remote_copy(
            src_ref=sums.at[src], dst_ref=sums.at[src],
            send_sem=sum_send.at[d], recv_sem=sum_recv.at[src],
            device_id={"frame": fr}, device_id_type=MESH,
        ).wait_recv()

    each(m - 1, sum_arrivals)

    def scatter(g):
        both = sums[0, g]
        for f in range(1, m):
            both = both + sums[f, g]
        num = both[0:GROUP]
        den = jnp.sum(jnp.where(own_lane, both[GROUP : GROUP + 1], 0.0), axis=1, keepdims=True)
        wf = w_mine[g]
        four = parts(num * wf, 2) + parts(den * wf, 2)
        idx = vidx_ref[at(g, GROUP), :]
        lane = lax.bitwise_and(idx, LANES - 1)
        for o in range(GROUP):
            hit = lax.broadcasted_iota(I32, (LANES, LANES), 0) == lane[o : o + 1, :]
            for k in range(4):
                col_val[k * LANES : (k + 1) * LANES, o * LANES : (o + 1) * LANES] = jnp.where(
                    hit, four[k][o : o + 1, :], 0.0
                ).astype(BF16)
        return dot_nt(row_hot[...], col_val[...])

    def finish(acc):
        num = acc[:, 0:LANES] + acc[:, LANES : 2 * LANES]
        den = acc[:, 2 * LANES : 3 * LANES] + acc[:, 3 * LANES : 4 * LANES]
        newv_ref[...] = (num + prior_weight * vol_ref[...]) / (den + prior_weight)

    if total == GROUP:
        finish(scatter(0))
    else:
        acc_scr[...] = scatter(0)

        def more(g, _):
            hot_rows(g)
            acc_scr[...] += scatter(g)
            return 0

        lax.fori_loop(1, total // GROUP, more, 0)
        finish(acc_scr[...])

    each(n - 1, lambda d: val_copy(d).wait_send())
    each(n - 1, lambda d: pw_copy(d).wait_send())
    each(n - 1, lambda d: score_copy(d).wait_send())
    each(m - 1, lambda d: sum_copy(d).wait_send())


def hand_out(vol_ref, probs_ref, vol_out, probs_out, sem):
    copies = [
        pltpu.make_async_copy(vol_ref, vol_out, sem.at[0]),
        pltpu.make_async_copy(probs_ref, probs_out, sem.at[1]),
    ]
    for c in copies:
        c.start()
    for c in copies:
        c.wait()


def on_device(n, m, volume, voxel_index, pixel_index, weights, background, counts):
    local, columns = pixel_index.shape
    total, entries = voxel_index.shape
    frames, pixels = counts.shape
    pix_rows = pixels // LANES
    vox_rows = volume.shape[0] // LANES
    groups = total // GROUP
    vmem = pl.BlockSpec(memory_space=pltpu.VMEM)
    hbm = pl.BlockSpec(memory_space=pltpu.MemorySpace.HBM)
    dma = pltpu.SemaphoreType.DMA
    new_volume, probs = pl.pallas_call(
        functools.partial(kernel, n, m),
        out_shape=(
            pltpu.VMEM((vox_rows, LANES), F32),
            pltpu.VMEM((local, frames), F32),
        ),
        in_specs=[hbm] * 6,
        out_specs=(vmem, vmem),
        scratch_shapes=[
            pltpu.VMEM((vox_rows, LANES), F32),
            pltpu.VMEM((total, entries), I32),
            pltpu.VMEM((local, columns), I32),
            pltpu.VMEM((local, columns), BF16),
            pltpu.VMEM((pix_rows, LANES), F32),
            pltpu.VMEM((frames, pixels), I32),
            pltpu.VMEM((frames, pixels), BF16),
            pltpu.VMEM((n, local, LANES), F32),
            pltpu.VMEM((n, local, LANES), F32),
            pltpu.VMEM((n, 2 * local, LANES), F32),
            pltpu.VMEM((n, 2 * local, LANES), F32),
            pltpu.VMEM((local, LANES, columns), BF16),
            pltpu.VMEM((local, 3 * pix_rows, columns), BF16),
            pltpu.VMEM((8, pixels), F32),
            pltpu.VMEM((local, frames), F32),
            pltpu.VMEM((n, local, frames), F32),
            pltpu.VMEM((groups, GROUP, LANES), I32),
            pltpu.VMEM((groups, GROUP, LANES), F32),
            pltpu.VMEM((vox_rows, GROUP * LANES), BF16),
            pltpu.VMEM((4 * LANES, GROUP * LANES), BF16),
            pltpu.VMEM((m, groups, GROUP + 8, LANES), F32),
            pltpu.VMEM((vox_rows if groups > 1 else 8, 4 * LANES), F32),
            dma((5,)), dma((CHUNKS,)),
            dma((n,)), dma((n,)), dma((n,)), dma((n,)), dma((n,)), dma((n,)),
            dma((m,)), dma((m,)),
        ],
        compiler_params=pltpu.CompilerParams(
            collective_id=0, has_side_effects=True, vmem_limit_bytes=VMEM_ALL - 4 * (vox_rows * LANES + local * frames) - LEFT
        ),
    )(
        volume.reshape(vox_rows, LANES), voxel_index, pixel_index, weights,
        background.reshape(pix_rows, LANES), counts,
    )
    new_volume, probs = pl.pallas_call(
        hand_out,
        out_shape=(
            jax.ShapeDtypeStruct(new_volume.shape, F32),
            jax.ShapeDtypeStruct(probs.shape, F32),
        ),
        in_specs=[vmem] * 2,
        out_specs=[pl.BlockSpec(memory_space=pl.ANY)] * 2,
        scratch_shapes=[dma((2,))],
        compiler_params=pltpu.CompilerParams(vmem_limit_bytes=1024 * 1024),
    )(new_volume, probs)
    return (new_volume.reshape(-1), probs)


def solution(mesh):
    n, m = mesh.shape["orient"], mesh.shape["frame"]
    in_specs = (
        P("orient"),
        P(None, "orient"),
        P("orient", None),
        P("orient", None),
        P(),
        P("frame", None),
    )
    out_specs = (P("orient"), P("orient", "frame"))
    return jax.shard_map(
        functools.partial(on_device, n, m), mesh=mesh, in_specs=in_specs, out_specs=out_specs, check_vma=False
    )
```

```python
import functools

import jax
import jax.numpy as jnp
from jax import lax
from jax.experimental import pallas as pl
from jax.experimental.pallas import tpu as pltpu
from jax.sharding import PartitionSpec as P

prior_weight = 0.05
LANES = 128
VMEM_ALL = 64 * 1024 * 1024
LEFT = 256 * 1024
GROUP = 16
CHUNKS = 4
MESH = pl.DeviceIdType.MESH
F32, BF16, I32 = jnp.float32, jnp.bfloat16, jnp.int32


def each(count, body):
    if count <= 16:
        for i in range(count):
            body(i)
    else:
        lax.fori_loop(0, count, lambda i, _: (body(i), 0)[1], 0)


def at(i, size):
    return pl.ds(i * size if isinstance(i, int) else pl.multiple_of(i * size, size), size)


def parts(x, count):
    out = []
    for _ in range(count):
        p = x.astype(BF16).astype(F32)
        out.append(p)
        x = x - p
    return out


def dot_nt(a, b):
    return lax.dot_general(a, b, (((1,), (1,)), ((), ())), preferred_element_type=F32)


def lane_pick(rows, lane):
    return jnp.take_along_axis(rows, lane, axis=1, mode="promise_in_bounds")


def kernel(
    n, m,
    vol_hbm, vidx_hbm, pix_hbm, w_hbm, bg_hbm, cnt_ref,
    newv_ref, probs_ref,
    vol_ref, vidx_ref, pix_ref, w_ref, bg_ref,
    cnt_i, cnt_b, vals, got_vals, pw, got_pw, pix_hot, spread, logs, scores, all_scores,
    pix_mine, w_mine, row_hot, col_val, sums, acc_scr,
    in_sem, cnt_sem, val_send, val_recv, pw_send, pw_recv, sc_send, sc_recv, sum_send, sum_recv,
):
    me = lax.axis_index("orient")
    fr = lax.axis_index("frame")
    local = pix_hbm.shape[0]
    total = n * local
    frames, pixels = cnt_ref.shape
    pix_rows = pixels // LANES
    vox_rows = vol_ref.shape[0]
    step = frames // CHUNKS
    per_group = GROUP // local

    barrier = pltpu.get_barrier_semaphore()

    def greet_o(d):
        pl.semaphore_signal(barrier, inc=1, device_id={"orient": lax.rem(me + d + 1, n)}, device_id_type=MESH)

    def greet_f(d):
        pl.semaphore_signal(barrier, inc=1, device_id={"frame": lax.rem(fr + d + 1, m)}, device_id_type=MESH)

    small = [
        pltpu.make_async_copy(src, dst, in_sem.at[i])
        for i, (src, dst) in enumerate(
            [
                (vidx_hbm, vidx_ref), (vol_hbm, vol_ref), (pix_hbm, pix_ref),
                (w_hbm, w_ref), (bg_hbm, bg_ref),
            ]
        )
    ]
    each(n - 1, greet_o)
    each(m - 1, greet_f)
    for c in small:
        c.start()

    loads = [
        pltpu.make_async_copy(
            cnt_ref.at[pl.ds(i * step, step)], cnt_i.at[pl.ds(i * step, step)], cnt_sem.at[i]
        )
        for i in range(CHUNKS)
    ]
    for c in loads:
        c.start()
    for c in small:
        c.wait()

    def gather_group(g):
        idx = vidx_ref[at(g, GROUP), :]
        row = lax.shift_right_logical(idx, 7)
        lane = lax.bitwise_and(idx, LANES - 1)

        def body(t, acc):
            base = pl.multiple_of(t * 8, 8)
            block = vol_ref[pl.ds(base, 8), :]
            for i in range(8):
                line = jnp.broadcast_to(block[i : i + 1, :], (GROUP, LANES))
                acc = jnp.where(row == base + i, lane_pick(line, lane), acc)
            return acc

        acc = lax.fori_loop(0, vox_rows // 8, body, jnp.zeros((GROUP, LANES), F32), unroll=2)
        for j in range(per_group):
            vals[g * per_group + j] = acc[j * local : (j + 1) * local, :]

    each(total // GROUP, gather_group)

    def fill_pw(j):
        pw[j, 0:local] = pix_ref[:, at(j, LANES)].astype(F32)
        pw[j, local : 2 * local] = w_ref[:, at(j, LANES)].astype(F32)

    each(n, fill_pw)

    pl.semaphore_wait(barrier, n + m - 2)

    def val_copy(d):
        to = lax.rem(me + d + 1, n)
        return pltpu.make_async_remote_copy(
            src_ref=vals.at[to], dst_ref=got_vals.at[me],
            send_sem=val_send.at[d], recv_sem=val_recv.at[me],
            device_id={"orient": to}, device_id_type=MESH,
        )

    def pw_copy(d):
        to = lax.rem(me + d + 1, n)
        return pltpu.make_async_remote_copy(
            src_ref=pw.at[to], dst_ref=got_pw.at[me],
            send_sem=pw_send.at[d], recv_sem=pw_recv.at[me],
            device_id={"orient": to}, device_id_type=MESH,
        )

    def score_copy(d):
        to = lax.rem(me + d + 1, n)
        return pltpu.make_async_remote_copy(
            src_ref=scores, dst_ref=all_scores.at[me],
            send_sem=sc_send.at[d], recv_sem=sc_recv.at[me],
            device_id={"orient": to}, device_id_type=MESH,
        )

    def sum_copy(d):
        to = lax.rem(fr + d + 1, m)
        return pltpu.make_async_remote_copy(
            src_ref=sums.at[fr], dst_ref=sums.at[fr],
            send_sem=sum_send.at[d], recv_sem=sum_recv.at[fr],
            device_id={"frame": to}, device_id_type=MESH,
        )

    def arrivals(buffer, sems, own, count, send_sems):
        def body(d):
            src = lax.rem(own + d + 1, count)
            pltpu.make_async_remote_copy(
                src_ref=buffer.at[src], dst_ref=buffer.at[src],
                send_sem=send_sems.at[d], recv_sem=sems.at[src],
                device_id={"orient": me}, device_id_type=MESH,
            ).wait_recv()

        each(count - 1, body)

    each(n - 1, lambda d: val_copy(d).start())
    each(n - 1, lambda d: pw_copy(d).start())
    got_vals[me] = vals[me]
    got_pw[me] = pw[me]

    def hot_pix(s):
        for o in range(local):
            lane = lax.bitwise_and(pix_ref[pl.ds(o, 1), at(s, LANES)], LANES - 1)
            hot = lax.broadcasted_iota(I32, (LANES, LANES), 0) == lane
            pix_hot[o, :, at(s, LANES)] = jnp.where(hot, 1.0, 0.0).astype(BF16)

    each(n, hot_pix)

    for i in range(CHUNKS):
        loads[i].wait()

        def cast(t, _, i=i):
            rows = pl.ds(pl.multiple_of(i * step + t * 16, 16), 16)
            cnt_b[rows, :] = cnt_i[rows, :].astype(F32).astype(BF16)
            return 0

        lax.fori_loop(0, step // 16, cast, 0)

    arrivals(got_vals, val_recv, me, n, val_send)

    def spread_slab(s):
        contrib = got_vals[s] * pw[s, local : 2 * local]
        for o in range(local):
            row = lax.shift_right_logical(pix_ref[pl.ds(o, 1), at(s, LANES)], 7)
            hit = lax.broadcasted_iota(I32, (pix_rows, LANES), 0) == row
            for k, part in enumerate(parts(contrib[o : o + 1, :], 3)):
                spread[o, k * pix_rows : (k + 1) * pix_rows, at(s, LANES)] = jnp.where(hit, part, 0.0).astype(BF16)

    each(n, spread_slab)

    logs[...] = jnp.zeros_like(logs)
    slice_sums = []
    for o in range(local):
        d3 = dot_nt(spread[o], pix_hot[o])
        sl = d3[0:pix_rows] + d3[pix_rows : 2 * pix_rows] + d3[2 * pix_rows : 3 * pix_rows] + bg_ref[...]
        slice_sums.append(jnp.sum(jnp.sum(sl, axis=1, keepdims=True), axis=0, keepdims=True))
        lg = jnp.log(sl)
        for r in range(pix_rows):
            logs[o : o + 1, r * LANES : (r + 1) * LANES] = lg[r : r + 1, :]
    pad = logs.shape[0]
    lv = logs[...]
    stack = jnp.concatenate(parts(lv, 3) + [jnp.zeros_like(lv)], axis=0).astype(BF16)
    quarter = pixels // 4
    ll = [
        dot_nt(stack[:, q * quarter : (q + 1) * quarter], cnt_b[:, q * quarter : (q + 1) * quarter])
        for q in range(4)
    ]
    ll = (ll[0] + ll[1]) + (ll[2] + ll[3])
    ll = ll[0:pad] + ll[pad : 2 * pad] + ll[2 * pad : 3 * pad]
    scores[...] = (64.0 / pixels) * (ll[0:local] - jnp.concatenate(slice_sums, axis=0))
    each(n - 1, lambda d: score_copy(d).start())
    all_scores[me] = scores[...]

    arrivals(got_pw, pw_recv, me, n, pw_send)

    def unpack(g):
        for j in range(per_group):
            src = got_pw[g * per_group + j]
            pix_mine[g, j * local : (j + 1) * local] = src[0:local].astype(I32)
            w_mine[g, j * local : (j + 1) * local] = src[local : 2 * local]

    each(total // GROUP, unpack)

    def hot_rows(g):
        idx = vidx_ref[at(g, GROUP), :]
        for o in range(GROUP):
            row = lax.shift_right_logical(idx[o : o + 1, :], 7)
            hit = lax.broadcasted_iota(I32, (vox_rows, LANES), 0) == row
            row_hot[:, o * LANES : (o + 1) * LANES] = jnp.where(hit, 1.0, 0.0).astype(BF16)

    hot_rows(0)

    arrivals(all_scores, sc_recv, me, n, sc_send)
    top = jnp.max(jnp.max(all_scores[...], axis=0), axis=0, keepdims=True)
    whole_sum = jnp.sum(jnp.sum(jnp.exp(all_scores[...] - top[None]), axis=0), axis=0, keepdims=True)

    own_lane = lax.broadcasted_iota(I32, (GROUP, LANES), 0) == lax.broadcasted_iota(I32, (GROUP, LANES), 1)

    def numerators(g):
        pieces = [
            jnp.exp(all_scores[g * per_group + j] - top) / whole_sum for j in range(per_group)
        ]
        pr = jnp.concatenate(pieces, axis=0)
        den = jnp.sum(pr, axis=1, keepdims=True)
        two = jnp.concatenate(parts(pr, 2), axis=0).astype(BF16)
        pix = pix_mine[g]
        row = lax.shift_right_logical(pix, 7)
        lane = lax.bitwise_and(pix, LANES - 1)
        acc = jnp.zeros((GROUP, LANES), F32)
        wide = 4
        for q in range(pix_rows // wide):
            d2 = jnp.dot(
                two, cnt_b[:, q * wide * LANES : (q + 1) * wide * LANES], preferred_element_type=F32
            )
            num = d2[0:GROUP] + d2[GROUP : 2 * GROUP]
            for i in range(wide):
                got = lane_pick(num[:, i * LANES : (i + 1) * LANES], lane)
                acc = jnp.where(row == q * wide + i, got, acc)
        sums[fr, g, 0:GROUP] = acc
        sums[fr, g, GROUP:] = jnp.broadcast_to(
            jnp.sum(jnp.where(own_lane, den, 0.0), axis=0, keepdims=True), (8, LANES)
        )

    each(total // GROUP, numerators)
    each(m - 1, lambda d: sum_copy(d).start())
    probs_ref[...] = jnp.exp(scores[...] - top) / whole_sum

    def sum_arrivals(d):
        src = lax.rem(fr + d + 1, m)
        pltpu.make_async_remote_copy(
            src_ref=sums.at[src], dst_ref=sums.at[src],
            send_sem=sum_send.at[d], recv_sem=sum_recv.at[src],
            device_id={"frame": fr}, device_id_type=MESH,
        ).wait_recv()

    each(m - 1, sum_arrivals)

    def scatter(g):
        both = sums[0, g]
        for f in range(1, m):
            both = both + sums[f, g]
        num = both[0:GROUP]
        den = jnp.sum(jnp.where(own_lane, both[GROUP : GROUP + 1], 0.0), axis=1, keepdims=True)
        wf = w_mine[g]
        four = parts(num * wf, 2) + parts(den * wf, 2)
        idx = vidx_ref[at(g, GROUP), :]
        lane = lax.bitwise_and(idx, LANES - 1)
        for o in range(GROUP):
            hit = lax.broadcasted_iota(I32, (LANES, LANES), 0) == lane[o : o + 1, :]
            for k in range(4):
                col_val[k * LANES : (k + 1) * LANES, o * LANES : (o + 1) * LANES] = jnp.where(
                    hit, four[k][o : o + 1, :], 0.0
                ).astype(BF16)
        half = 2 * LANES
        return jnp.concatenate(
            [dot_nt(row_hot[...], col_val[0:half]), dot_nt(row_hot[...], col_val[half:])], axis=1
        )

    def finish(acc):
        num = acc[:, 0:LANES] + acc[:, LANES : 2 * LANES]
        den = acc[:, 2 * LANES : 3 * LANES] + acc[:, 3 * LANES : 4 * LANES]
        newv_ref[...] = (num + prior_weight * vol_ref[...]) / (den + prior_weight)

    if total == GROUP:
        finish(scatter(0))
    else:
        acc_scr[...] = scatter(0)

        def more(g, _):
            hot_rows(g)
            acc_scr[...] += scatter(g)
            return 0

        lax.fori_loop(1, total // GROUP, more, 0)
        finish(acc_scr[...])

    each(n - 1, lambda d: val_copy(d).wait_send())
    each(n - 1, lambda d: pw_copy(d).wait_send())
    each(n - 1, lambda d: score_copy(d).wait_send())
    each(m - 1, lambda d: sum_copy(d).wait_send())


def hand_out(vol_ref, probs_ref, vol_out, probs_out, sem):
    copies = [
        pltpu.make_async_copy(vol_ref, vol_out, sem.at[0]),
        pltpu.make_async_copy(probs_ref, probs_out, sem.at[1]),
    ]
    for c in copies:
        c.start()
    for c in copies:
        c.wait()


def on_device(n, m, volume, voxel_index, pixel_index, weights, background, counts):
    local, columns = pixel_index.shape
    total, entries = voxel_index.shape
    frames, pixels = counts.shape
    pix_rows = pixels // LANES
    vox_rows = volume.shape[0] // LANES
    groups = total // GROUP
    vmem = pl.BlockSpec(memory_space=pltpu.VMEM)
    hbm = pl.BlockSpec(memory_space=pltpu.MemorySpace.HBM)
    dma = pltpu.SemaphoreType.DMA
    new_volume, probs = pl.pallas_call(
        functools.partial(kernel, n, m),
        out_shape=(
            pltpu.VMEM((vox_rows, LANES), F32),
            pltpu.VMEM((local, frames), F32),
        ),
        in_specs=[hbm] * 6,
        out_specs=(vmem, vmem),
        scratch_shapes=[
            pltpu.VMEM((vox_rows, LANES), F32),
            pltpu.VMEM((total, entries), I32),
            pltpu.VMEM((local, columns), I32),
            pltpu.VMEM((local, columns), BF16),
            pltpu.VMEM((pix_rows, LANES), F32),
            pltpu.VMEM((frames, pixels), I32),
            pltpu.VMEM((frames, pixels), BF16),
            pltpu.VMEM((n, local, LANES), F32),
            pltpu.VMEM((n, local, LANES), F32),
            pltpu.VMEM((n, 2 * local, LANES), F32),
            pltpu.VMEM((n, 2 * local, LANES), F32),
            pltpu.VMEM((local, LANES, columns), BF16),
            pltpu.VMEM((local, 3 * pix_rows, columns), BF16),
            pltpu.VMEM((8, pixels), F32),
            pltpu.VMEM((local, frames), F32),
            pltpu.VMEM((n, local, frames), F32),
            pltpu.VMEM((groups, GROUP, LANES), I32),
            pltpu.VMEM((groups, GROUP, LANES), F32),
            pltpu.VMEM((vox_rows, GROUP * LANES), BF16),
            pltpu.VMEM((4 * LANES, GROUP * LANES), BF16),
            pltpu.VMEM((m, groups, GROUP + 8, LANES), F32),
            pltpu.VMEM((vox_rows if groups > 1 else 8, 4 * LANES), F32),
            dma((5,)), dma((CHUNKS,)),
            dma((n,)), dma((n,)), dma((n,)), dma((n,)), dma((n,)), dma((n,)),
            dma((m,)), dma((m,)),
        ],
        compiler_params=pltpu.CompilerParams(
            collective_id=0, has_side_effects=True, vmem_limit_bytes=VMEM_ALL - 4 * (vox_rows * LANES + local * frames) - LEFT
        ),
    )(
        volume.reshape(vox_rows, LANES), voxel_index, pixel_index, weights,
        background.reshape(pix_rows, LANES), counts,
    )
    new_volume, probs = pl.pallas_call(
        hand_out,
        out_shape=(
            jax.ShapeDtypeStruct(new_volume.shape, F32),
            jax.ShapeDtypeStruct(probs.shape, F32),
        ),
        in_specs=[vmem] * 2,
        out_specs=[pl.BlockSpec(memory_space=pl.ANY)] * 2,
        scratch_shapes=[dma((2,))],
        compiler_params=pltpu.CompilerParams(vmem_limit_bytes=1024 * 1024),
    )(new_volume, probs)
    return (new_volume.reshape(-1), probs)


def solution(mesh):
    n, m = mesh.shape["orient"], mesh.shape["frame"]
    in_specs = (
        P("orient"),
        P(None, "orient"),
        P("orient", None),
        P("orient", None),
        P(),
        P("frame", None),
    )
    out_specs = (P("orient"), P("orient", "frame"))
    return jax.shard_map(
        functools.partial(on_device, n, m), mesh=mesh, in_specs=in_specs, out_specs=out_specs, check_vma=False
    )
```
